32 devices in a mesh: parts: 2 (over x), leaf: 16 (over z, y, core).
Axes of the slice: x: 2, y: 2, z: 4, core: 2. Of those that a mesh axis runs over, the one named last changes fastest.
Arguments:
- root_cov: float32 [6144, 3072], P(('parts', 'leaf')), parts along dimension 0, may hold values from -40 to 40, as said below
- panel_one: bfloat16 [6144, 2048], P(('parts', 'leaf')), parts along dimension 0, may hold values from -0.078125 to 0.078125
- pattern_one: int32 [24, 16], replicated, may hold values 0 or 1
- inv_one: float32 [4096, 2048], P('parts', 'leaf'), parts along dimension 0, may hold values from -40 to 40, as said below
- panel_parent: bfloat16 [4096, 1024], P(('parts', 'leaf')), parts along dimension 0, may hold values from -0.0625 to 0.0625
- panel_root: bfloat16 [6144, 1024], P(('parts', 'leaf')), parts along dimension 0, may hold values from -0.0625 to 0.0625
- pattern_two: int32 [40, 8], replicated, may hold values 0 or 1
- inv_two: float32 [2048, 1024], P('parts', 'leaf'), parts along dimension 0, may hold values from -40 to 40, as said below
Outputs:
- cross_one: float32 [6144, 2048], P(('parts', 'leaf')), parts along dimension 0
- cov_one: float32 [4096, 2048], P('parts', 'leaf'), parts along dimension 0
- cross_two_parent: float32 [4096, 1024], P(('parts', 'leaf')), parts along dimension 0
- cross_two_root: float32 [6144, 1024], P(('parts', 'leaf')), parts along dimension 0
- cov_two: float32 [2048, 1024], P('parts', 'leaf'), parts along dimension 0
The draws below stay inside these ranges and needn't reach their ends.
There are 2 independent parts, one for each index of `parts`. The reference program is written for one: setup_inputs(seed, part) draws one part's arguments, and reference() takes and returns one part's arrays. A program takes and returns all parts, laid end to end along the dimension named above; an argument that names none is the same for every part. Nothing has to cross between parts.
Inputs may be any that keep to these rules, and one draw needn't show every extreme that they name: `root_cov`: symmetric. `inv_one`: symmetric. `inv_two`: symmetric.
All inputs are finite; a program needn't handle non-finite values.
Results may differ from the reference program's by a relative error of at most 0.00095.
Values may be sent and summed in bfloat16 or wider, within the bound.
A program may use at most 128 MiB of HBM per device.

```python
import math
import jax
import jax.numpy as jnp
from jax import lax

C0 = 3072
C1 = 2048
C2 = 1024
BLOCK = 128


def assemble(key, noise, top):
    order = noise.shape[0]
    key_scale, key_bump = jax.random.split(key)
    logs = jax.random.uniform(key_scale, (order,), jnp.float32, 0.0, 0.5 * math.log(top))
    scales = jnp.exp(logs)
    bump = jax.random.uniform(key_bump, (order,), jnp.float32, 0.0, 1.0)
    symmetric = (noise + noise.T) * (0.6 / math.sqrt(2.0 * order))
    core = symmetric + jnp.diag(1.0 + bump)
    return scales[:, None] * core * scales[None, :]


def draw_root_cov(key, part):
    key = jax.random.fold_in(key, 11)
    key_noise, key_rest = jax.random.split(key)
    noise = jax.random.truncated_normal(key_noise, -4.0, 4.0, (C0, C0), jnp.float32)
    return assemble(key_rest, noise, 10.0)


def draw_inv_one(key, part):
    key = jax.random.fold_in(key, 12)
    key_noise, key_rest = jax.random.split(key)
    noise = jax.random.truncated_normal(key_noise, -4.0, 4.0, (C1, C1), jnp.float32)
    return assemble(key_rest, noise, 10.0)


def draw_inv_two(key, part):
    key = jax.random.fold_in(key, 13)
    key_noise, key_rest = jax.random.split(key)
    noise = jax.random.truncated_normal(key_noise, -4.0, 4.0, (C2, C2), jnp.float32)
    return assemble(key_rest, noise, 10.0)


def plant(values, stream_key, low, largest):
    longest = values.shape.index(max(values.shape))
    spots = []
    for shift in (0, 1):
        where = [jax.random.randint(jax.random.fold_in(stream_key, axis), (), 0, length) for axis, length in enumerate(values.shape)]
        where[longest] = (where[longest] + shift) % values.shape[longest]
        spots.append(tuple(where))
    return values.at[spots[0]].set(low).at[spots[1]].set(largest)


def shard_levels(stream_key, extent, cuts, least, largest):
    def one(dim, blocks):
        heights = jax.random.uniform(jax.random.fold_in(jax.random.fold_in(stream_key, 6), dim), (blocks,), jnp.float32, least / len(cuts), largest / len(cuts))
        return jnp.repeat(jnp.exp(heights), extent[dim] // blocks).reshape((-1,) + (1,) * (len(extent) - dim - 1))

    level = one(*cuts[0])
    for cut in cuts[1:]:
        level = level * one(*cut)
    return level


def centred(rng, dims, deviation, most, shards=(), kind=jnp.bfloat16):
    loudness = shard_levels(rng, dims, shards, -0.22, 0.18) if shards else 1.0
    array = jax.random.normal(rng, dims, jnp.float32) * deviation * loudness
    return jnp.minimum(jnp.maximum(array, -most), most).astype(kind)


def setup_inputs(seed: int = 0, part: int = 0) -> dict:
    key_list = jax.random.split(jax.random.key(seed), 9)
    part_keys = jax.random.split(jax.random.fold_in(key_list[8], part), 9)
    return {
        "root_cov": draw_root_cov(jax.random.fold_in(jax.random.fold_in(key_list[8], part), 71), part),
        "panel_one": centred(part_keys[1], (C0, C1), (2 * C0) ** -0.5, 0.078125, ((0, 16),)),
        "pattern_one": plant((jax.random.randint(key_list[2], (C0 // BLOCK, C1 // BLOCK), 0, 2) < 1).astype(jnp.int32), jax.random.fold_in(key_list[2], 1), 0, 1),
        "inv_one": draw_inv_one(jax.random.fold_in(jax.random.fold_in(key_list[8], part), 71), part),
        "panel_parent": centred(part_keys[4], (C1, C2), (2 * (C0 + C1)) ** -0.5, 0.0625, ((0, 16),)),
        "panel_root": centred(part_keys[5], (C0, C2), (2 * (C0 + C1)) ** -0.5, 0.0625, ((0, 16),)),
        "pattern_two": plant((jax.random.randint(key_list[6], ((C1 + C0) // BLOCK, C2 // BLOCK), 0, 2) < 1).astype(jnp.int32), jax.random.fold_in(key_list[6], 1), 0, 1),
        "inv_two": draw_inv_two(jax.random.fold_in(jax.random.fold_in(key_list[8], part), 71), part),
    }


def expand_tiles(pattern):
    return jnp.repeat(jnp.repeat(pattern, BLOCK, axis=0), BLOCK, axis=1) > 0


def product(left, right):
    return jnp.dot(left, right, precision=lax.Precision.HIGHEST, preferred_element_type=jnp.float32)


def reference(root_cov, panel_one, pattern_one, inv_one, panel_parent, panel_root, pattern_two, inv_two):
    masked_one = jnp.where(expand_tiles(pattern_one), panel_one, jnp.zeros_like(panel_one))
    keep_two = expand_tiles(pattern_two)
    masked_parent = jnp.where(keep_two[:C1], panel_parent, jnp.zeros_like(panel_parent))
    masked_root = jnp.where(keep_two[C1:], panel_root, jnp.zeros_like(panel_root))
    one_wide = masked_one.astype(jnp.float32)
    parent_wide = masked_parent.astype(jnp.float32)
    root_wide = masked_root.astype(jnp.float32)
    cross_one = -product(root_cov, one_wide)
    cov_one = inv_one - product(one_wide.T, cross_one)
    cross_two_parent = -(product(cov_one.T, parent_wide) + product(cross_one.T, root_wide))
    cross_two_root = -(product(cross_one, parent_wide) + product(root_cov, root_wide))
    cov_two = inv_two - (product(parent_wide.T, cross_two_parent) + product(root_wide.T, cross_two_root))
    return cross_one, cov_one, cross_two_parent, cross_two_root, cov_two
```

```python
import jax
import jax.numpy as jnp
from jax import lax
from jax.experimental import pallas as pl
from jax.experimental.pallas import tpu as pltpu
from jax.sharding import PartitionSpec as P

BLOCK = 128


def product(left, right):
    return jnp.dot(left, right, precision=lax.Precision.HIGHEST, preferred_element_type=jnp.float32)


def contract_rows(left, right):
    return lax.dot_general(
        left,
        right,
        (((0,), (0,)), ((), ())),
        precision=lax.Precision.HIGHEST,
        preferred_element_type=jnp.float32,
    )


def pattern_rows(pattern, first_row, count_rows):
    row_index = first_row + jnp.arange(count_rows, dtype=jnp.int32)
    tile_index = row_index // BLOCK
    choose = (tile_index[:, None] == jnp.arange(pattern.shape[0], dtype=jnp.int32)[None, :]).astype(
        jnp.float32
    )
    picked = jnp.dot(choose, pattern.astype(jnp.float32))
    return jnp.repeat(picked, BLOCK, axis=1) > 0.5


def per_device(
    root_cov, panel_one, pattern_one, inv_one, panel_parent, panel_root, pattern_two, inv_two
):
    position = lax.axis_index("leaf")
    root_rows = root_cov.shape[0]
    parent_rows = panel_parent.shape[0]
    parent_width = panel_one.shape[1]
    keep_one = pattern_rows(pattern_one, position * root_rows, root_rows)
    masked_one = jnp.where(keep_one, panel_one, jnp.zeros_like(panel_one))
    keep_parent = pattern_rows(pattern_two, position * parent_rows, parent_rows)
    masked_parent = jnp.where(keep_parent, panel_parent, jnp.zeros_like(panel_parent))
    keep_root = pattern_rows(pattern_two, parent_width + position * root_rows, root_rows)
    masked_root = jnp.where(keep_root, panel_root, jnp.zeros_like(panel_root))
    full_one, full_parent, full_root = (
        lax.all_gather(masked_one, "leaf", axis=0, tiled=True),
        lax.all_gather(masked_parent, "leaf", axis=0, tiled=True),
        lax.all_gather(masked_root, "leaf", axis=0, tiled=True),
    )
    one_wide = full_one.astype(jnp.float32)
    cross_rows = -product(root_cov, one_wide)
    cross_cols = lax.all_to_all(cross_rows, "leaf", split_axis=1, concat_axis=0, tiled=True)
    cov_cols = inv_one - contract_rows(one_wide, cross_cols)
    parent_wide = full_parent.astype(jnp.float32)
    root_wide = full_root.astype(jnp.float32)
    upper_rows = -(contract_rows(cov_cols, parent_wide) + contract_rows(cross_cols, root_wide))
    lower_rows = -(product(cross_rows, parent_wide) + product(root_cov, root_wide))
    upper_cols, lower_cols = (
        lax.all_to_all(
            upper_rows.astype(jnp.bfloat16), "leaf", split_axis=1, concat_axis=0, tiled=True
        ).astype(upper_rows.dtype),
        lax.all_to_all(
            lower_rows.astype(jnp.bfloat16), "leaf", split_axis=1, concat_axis=0, tiled=True
        ).astype(lower_rows.dtype),
    )
    child_cov = inv_two - (
        contract_rows(parent_wide, upper_cols) + contract_rows(root_wide, lower_cols)
    )
    return (cross_rows, cov_cols, upper_rows, lower_rows, child_cov)


PLANES = 4
GROUP = PLANES * 4
COLUMN_TILE = 512
CUTS = (2, 1, 1)
CROSS_SCALE = 4.0


def split_rows(values):
    high = values.astype(jnp.bfloat16)
    low = (values - high.astype(jnp.float32)).astype(jnp.bfloat16)
    return high, low


def split_wide(values):
    high = lax.reduce_precision(values, 8, 7)
    return high.astype(jnp.bfloat16), (values - high).astype(jnp.bfloat16)


def gather_steps(shards, patterns, tiles_before, fulls, outs, cuts, send_sem, recv_sem, out_sem, use):
    leaf = lax.axis_index("leaf")
    plane, side, core = leaf // 4, (leaf // 2) % 2, leaf % 2

    def device(z, y, c):
        return z * 4 + y * 2 + c

    up, down = device(plane + 1, side, core), device(plane - 1, side, core)
    across, twin = device(plane, 1 - side, core), device(plane, side, 1 - core)
    barrier = pltpu.get_barrier_semaphore()
    has_up, has_down = plane < PLANES - 1, plane > 0
    for there, target in ((has_up, up), (has_down, down), (None, across), (None, twin)):
        def greet(target=target):
            pl.semaphore_signal(
                barrier, inc=1, device_id={"leaf": target}, device_id_type=pl.DeviceIdType.MESH
            )
        if there is None:
            greet()
        else:
            pl.when(there)(greet)

    def rows_of(index, origin, count=1):
        height = shards[index].shape[0]
        return pl.ds(pl.multiple_of(origin * height, 16), height * count)

    for index, shard in enumerate(shards):
        height = shard.shape[0]
        tiles = patterns[index].shape[0]
        row = lax.broadcasted_iota(jnp.int32, (height, tiles), 0) + leaf * height
        tile = lax.broadcasted_iota(jnp.int32, (height, tiles), 1) - tiles_before[index]
        inside = (row >= tile * BLOCK) & (row < (tile + 1) * BLOCK)
        keep = jnp.dot(
            inside.astype(jnp.float32), patterns[index][...], preferred_element_type=jnp.float32
        )
        wide = shard[...].astype(jnp.float32)
        fulls[index][rows_of(index, leaf), :] = jnp.where(keep > 0.5, wide, 0.0).astype(jnp.bfloat16)
    pl.semaphore_wait(barrier, 2 + has_up.astype(jnp.int32) + has_down.astype(jnp.int32))

    started = []

    pieces = []
    for index, (full, parts) in enumerate(zip(fulls, cuts)):
        width = full.shape[1] // parts
        pieces += [(index, part * width, width) for part in range(parts)]

    def piece_copy(piece, origin, target, sem):
        index, first, width = pieces[piece]
        here = fulls[index].at[rows_of(index, origin), pl.ds(first, width)]
        return pltpu.make_async_remote_copy(
            src_ref=here,
            dst_ref=here,
            send_sem=send_sem.at[sem],
            recv_sem=recv_sem.at[piece, origin],
            device_id={"leaf": target},
            device_id_type=pl.DeviceIdType.MESH,
        )

    def relay(origin, targets, there=None, received=True):
        for piece in range(len(pieces)):
            if received:
                def wait(piece=piece):
                    piece_copy(piece, origin, twin, 0).wait_recv()
                wait() if there is None else pl.when(there)(wait)
            for target, when in targets:
                copy = piece_copy(piece, origin, target, len(started))
                started.append((when, copy))
                copy.start() if when is None else pl.when(when)(copy.start)

    stored = []

    def chip(z, y, there):
        def work():
            relay(device(z, y, 1 - core), ())
            for index, (full, out) in enumerate(zip(fulls, outs)):
                rows = rows_of(index, device(z, y, 0), 2)
                pltpu.make_async_copy(full.at[rows, :], out.at[rows, :], out_sem.at[index, z * 2 + y]).start()
            use(z * 2 + y)
        stored.append((there, z, y))
        if there is None:
            work()
        else:
            pl.when(there)(work)

    own = device(plane, side, core)
    relay(own, ((up, has_up), (down, has_down), (across, None), (twin, None)), received=False)

    def from_across(z, there):
        origin = device(z, 1 - side, core)
        onward = core == 1 if there is None else there & (core == 1)
        targets = (
            (down, onward & has_down & (z == PLANES - 1)),
            (up, onward & has_up & (z == 0)),
            (twin, there),
        )
        relay(origin, targets, there)

    for step in range(1, PLANES + 1):
        if step < PLANES:
            for z, there, onward, more in (
                (plane - step, plane - step >= 0, up, has_up),
                (plane + step, plane + step <= PLANES - 1, down, has_down),
            ):
                origin = device(z, side, core)
                far = there & ((core == 0) | ((z > 0) & (z < PLANES - 1)))
                relay(origin, ((onward, there & more), (across, far), (twin, there)), there)
        back = step - 1
        if back == 0:
            from_across(plane, None)
            chip(plane, side, None)
            chip(plane, 1 - side, None)
        else:
            near = (
                (plane - back, plane - back >= 0),
                (plane + back, plane + back <= PLANES - 1),
            )
            for z, there in near:
                from_across(z, there)
            for z, there in near:
                chip(z, side, there)
                chip(z, 1 - side, there)

    for there, copy in started:
        if there is None:
            copy.wait_send()
        else:
            pl.when(there)(copy.wait_send)
    for there, z, y in stored:
        def finish(z=z, y=y):
            for index, (full, out) in enumerate(zip(fulls, outs)):
                rows = rows_of(index, device(z, y, 0), 2)
                pltpu.make_async_copy(full.at[rows, :], out.at[rows, :], out_sem.at[index, z * 2 + y]).wait()
        if there is None:
            finish()
        else:
            pl.when(there)(finish)


def add_products(stacked, start, depth, full, full_start, total):
    height = total.shape[0]
    left = stacked[:, pl.ds(pl.multiple_of(start, BLOCK), depth)]

    def tile(step, carry):
        columns = pl.ds(pl.multiple_of(step * COLUMN_TILE, COLUMN_TILE), COLUMN_TILE)
        both = jnp.dot(
            left,
            full[pl.ds(pl.multiple_of(full_start, 16), depth), columns],
            preferred_element_type=jnp.float32,
        )
        total[:, columns] -= both[:height] + both[height:]
        return carry

    lax.fori_loop(0, total.shape[1] // COLUMN_TILE, tile, 0)


def fill_split(stacked, values):
    height = values.shape[0]
    high, low = split_rows(values[...])
    stacked[:height, :] = high
    stacked[height:, :] = low


def gather_kernel(
    root, one_shard, root_shard, parent_shard, one_pattern, two_pattern,
    cross, lower, one_out, root_out, parent_out,
    one_full, root_full, parent_full, stacked, cross_stacked, send_sem, recv_sem, out_sem,
):
    depth, width = 2 * root_shard.shape[0], parent_full.shape[0]
    fill_split(stacked, root)
    cross[...] = jnp.zeros_like(cross)
    lower[...] = jnp.zeros_like(lower)

    def use(block):
        add_products(stacked, block * depth, depth, one_full, block * depth, cross)
        add_products(stacked, block * depth, depth, root_full, block * depth, lower)

    gather_steps(
        (one_shard, root_shard, parent_shard),
        (one_pattern, two_pattern, two_pattern),
        (0, width // BLOCK, 0),
        (one_full, root_full, parent_full),
        (one_out, root_out, parent_out),
        CUTS, send_sem, recv_sem, out_sem, use,
    )
    fill_split(cross_stacked, cross)
    add_products(cross_stacked, 0, width, parent_full, 0, lower)


def vmem(count):
    return [pl.BlockSpec(memory_space=pltpu.VMEM)] * count


def semaphores(arrays, pieces):
    return [
        pltpu.SemaphoreType.DMA((48 * pieces,)),
        pltpu.SemaphoreType.DMA((pieces, GROUP)),
        pltpu.SemaphoreType.DMA((arrays, GROUP // 2)),
    ]


def params(collective_id):
    return pltpu.CompilerParams(
        collective_id=collective_id, has_side_effects=True, vmem_limit_bytes=54 * 1024 * 1024
    )


def estimate(flops, nbytes):
    return pl.CostEstimate(flops=flops, bytes_accessed=nbytes, transcendentals=0)


def contract_split(left, right):
    return lax.dot_general(
        left, right, (((0,), (0,)), ((), ())), preferred_element_type=jnp.float32
    )


def per_device_kernels(
    root_cov, panel_one, pattern_one, inv_one, panel_parent, panel_root, pattern_two, inv_two
):
    rows, order = root_cov.shape
    parent_width, child_width = panel_one.shape[1], panel_root.shape[1]
    bf16, f32 = jnp.bfloat16, jnp.float32
    any_space = pl.BlockSpec(memory_space=pl.ANY)
    spread_one = jnp.repeat(pattern_one.astype(f32), BLOCK, axis=1)
    spread_two = jnp.repeat(pattern_two.astype(f32), BLOCK, axis=1)
    cross_rows, lower_rows, full_one, full_root, full_parent = pl.pallas_call(
        gather_kernel,
        out_shape=(
            jax.ShapeDtypeStruct((rows, parent_width), f32),
            jax.ShapeDtypeStruct((rows, child_width), f32),
            jax.ShapeDtypeStruct((order, parent_width), bf16),
            jax.ShapeDtypeStruct((order, child_width), bf16),
            jax.ShapeDtypeStruct((parent_width, child_width), bf16),
        ),
        in_specs=vmem(6),
        out_specs=(*vmem(2), any_space, any_space, any_space),
        scratch_shapes=[
            pltpu.VMEM((order, parent_width), bf16),
            pltpu.VMEM((order, child_width), bf16),
            pltpu.VMEM((parent_width, child_width), bf16),
            pltpu.VMEM((2 * rows, order), bf16),
            pltpu.VMEM((2 * rows, parent_width), bf16),
        ] + semaphores(3, sum(CUTS)),
        compiler_params=params(0),
        cost_estimate=estimate(4 * rows * order * (parent_width + child_width), 300_000_000),
        name="gather_panels",
    )(root_cov, panel_one, panel_root, panel_parent, spread_one, spread_two)
    assert 3.125 * order * CROSS_SCALE < 65504
    cross_cols = lax.all_to_all(
        (cross_rows * CROSS_SCALE).astype(jnp.float16), "leaf", split_axis=1, concat_axis=0, tiled=True
    ).astype(f32) * (1.0 / CROSS_SCALE)
    lower_cols = lax.all_to_all(
        lower_rows.astype(bf16), "leaf", split_axis=1, concat_axis=0, tiled=True
    )
    width = cross_cols.shape[1]
    cross_two = jnp.concatenate(split_wide(cross_cols), axis=1)
    both = contract_split(full_one, cross_two)
    cov_cols = inv_one - (both[:, :width] + both[:, width:])
    cov_two = jnp.concatenate(split_wide(cov_cols), axis=1)
    both = contract_split(cov_two, full_parent) + contract_split(cross_two, full_root)
    upper_rows = -(both[:width] + both[width:])
    upper_cols = lax.all_to_all(
        upper_rows.astype(bf16), "leaf", split_axis=1, concat_axis=0, tiled=True
    )
    child_cov = inv_two - (
        contract_split(full_parent, upper_cols) + contract_split(full_root, lower_cols)
    )
    return (cross_rows, cov_cols, upper_rows, lower_rows, child_cov)


def solution(mesh):
    placed = (
        P(("parts", "leaf"), None),
        P(("parts", "leaf"), None),
        P(),
        P("parts", "leaf"),
        P(("parts", "leaf"), None),
        P(("parts", "leaf"), None),
        P(),
        P("parts", "leaf"),
    )
    return jax.shard_map(
        per_device_kernels if mesh.shape["leaf"] == GROUP else per_device,
        mesh=mesh,
        in_specs=placed,
        out_specs=(
            P(("parts", "leaf"), None),
            P("parts", "leaf"),
            P(("parts", "leaf"), None),
            P(("parts", "leaf"), None),
            P("parts", "leaf"),
        ),
        check_vma=False,
    )
```
